32 devices in a mesh: groups: 2 (over x), adapters: 4 (over y, core), tensor: 4 (over z).
Axes of the slice: x: 2, y: 2, z: 4, core: 2. Of those that a mesh axis runs over, the one named last changes fastest.
Arguments:
- hidden: bfloat16 [8192, 8192], P(('groups', 'adapters'), 'tensor'), parts along dimension 0, may hold values from -480 to 480
- input_norm_scale: bfloat16 [8192], P('tensor'), may hold values from 0.25 to 1.75
- key_value_weight: bfloat16 [8192, 2, 1024], P('tensor'), may hold values from -0.09375 to 0.09375
- adapter_down_weight: bfloat16 [64, 8192, 128], P(('groups', 'adapters'), 'tensor'), parts along dimension 0, may hold values from -0.0625 to 0.0625
- adapter_up_weight: bfloat16 [64, 2, 64, 1024], P(('groups', 'adapters')), parts along dimension 0, may hold values from -0.75 to 0.75
- request_adapter_index: int32 [128], P(('groups', 'adapters')), parts along dimension 0, may hold values from 0 to 31, as said below
- request_token_length: int32 [8, 16], P(('groups', 'adapters')), parts along dimension 0, may hold values from 1 to 128, 1024 in all within a row
- adapter_storage_row: int32 [64], P('groups'), parts along dimension 0, may hold values from 0 to 31, as said below
Outputs:
- keys: bfloat16 [8192, 1024], P(('groups', 'adapters'), 'tensor'), parts along dimension 0
- values: bfloat16 [8192, 1024], P(('groups', 'adapters'), 'tensor'), parts along dimension 0
The draws below stay inside these ranges and needn't reach their ends.
There are 2 independent parts, one for each index of `groups`. The reference program is written for one: setup_inputs(seed, part) draws one part's arguments, and reference() takes and returns one part's arrays. A program takes and returns all parts, laid end to end along the dimension named above; an argument that names none is the same for every part. Nothing has to cross between parts.
Inputs may be any that keep to these rules, and one draw needn't show every extreme that they name: `request_adapter_index`: the requests of one device may use adapters stored in many blocks of rows r * 8 to (r + 1) * 8 - 1, but at most 2 distinct adapters of any one block; every device's requests use exactly 2 distinct adapters of some block. A permutation: adapter a is stored at row adapter_storage_row[a] of adapter_down_weight and adapter_up_weight.
All inputs are finite; a program needn't handle non-finite values.
Results may differ from the reference program's by a relative error of at most 0.0049.
Values may be sent and summed in bfloat16 or wider, within the bound.
A program may use at most 128 MiB of HBM per device.

```python
import math
import jax
import jax.numpy as jnp
import numpy as np
from jax import lax

MODEL_WIDTH = 8192
KVH = 8
HD = 128
ADAPTER_RANK = 64
REQ_DEV = 16
TOK_DEV = 1024
ADP_DEV = 8
KEY_VALUE_WIDTH = 1024
LONGEST_REQUEST = 128
OWNERS = 4
ADAPTER_TOTAL = 32
REQUEST_TOTAL = 64
TOKEN_TOTAL = 4096


def plan(key):
    keys_all = jax.random.split(key, 10)
    storage = jax.random.permutation(keys_all[0], ADAPTER_TOTAL).astype(jnp.int32)
    owner_order = jax.random.permutation(keys_all[1], OWNERS).astype(jnp.int32)
    hot_first = jax.random.randint(keys_all[2], (OWNERS, 1), 0, ADP_DEV)
    hot_step = jax.random.randint(keys_all[3], (OWNERS, 1), 1, ADP_DEV)
    cold_first = jax.random.randint(keys_all[4], (OWNERS, OWNERS), 0, ADP_DEV)
    cold_step = jax.random.randint(keys_all[5], (OWNERS, OWNERS), 1, ADP_DEV)
    use_hot = jax.random.randint(keys_all[6], (OWNERS, OWNERS), 0, 2) == 1
    first_row = jnp.where(use_hot, hot_first, cold_first)
    second_row = (first_row + jnp.where(use_hot, hot_step, cold_step)) % ADP_DEV
    draws_one = jax.random.randint(keys_all[7], (OWNERS, REQ_DEV), 0, OWNERS)
    draws_two = jax.random.randint(keys_all[8], (OWNERS, REQ_DEV), 0, OWNERS)
    owner_pick = owner_order[jnp.minimum(draws_one, draws_two)]
    slot_keys = jax.random.split(keys_all[9], 3)
    slot_pick = jax.random.randint(slot_keys[0], (OWNERS, REQ_DEV), 0, 2)
    forced_first = jax.random.randint(slot_keys[1], (OWNERS, 1), 0, REQ_DEV)
    forced_second = (forced_first + jax.random.randint(slot_keys[2], (OWNERS, 1), 1, REQ_DEV)) % REQ_DEV
    request_index = jnp.arange(REQ_DEV, dtype=jnp.int32)[None, :]
    is_first = request_index == forced_first
    is_second = request_index == forced_second
    forced = jnp.logical_or(is_first, is_second)
    owner_pick = jnp.where(forced, owner_order[0], owner_pick)
    slot_pick = jnp.where(is_first, 0, jnp.where(is_second, 1, slot_pick))
    dest_index = jnp.arange(OWNERS, dtype=jnp.int32)[:, None]
    local_row = jnp.where(slot_pick == 0, first_row[owner_pick, dest_index], second_row[owner_pick, dest_index])
    adapter_ids = storage[owner_pick * ADP_DEV + local_row].reshape(-1).astype(jnp.int32)
    adapter_rows = jnp.argsort(storage).astype(jnp.int32)
    return (adapter_ids, adapter_rows)


def draw_request_adapter_index(key, part):
    adapter_ids, adapter_rows = plan(key)
    return adapter_ids


def draw_adapter_storage_row(key, part):
    adapter_ids, adapter_rows = plan(key)
    return adapter_rows


def draw_hidden(key, part):
    key = jax.random.fold_in(key, 7)
    keys_all = jax.random.split(key, 4)
    columns = jnp.arange(MODEL_WIDTH, dtype=jnp.float32)
    rising = jnp.exp(math.log(3.0) * columns / MODEL_WIDTH)
    column_scale = rising * jnp.exp(jax.random.uniform(keys_all[0], (MODEL_WIDTH,), minval=0.0, maxval=math.log(4.0)))
    values_base = jax.random.truncated_normal(keys_all[1], -4.0, 4.0, (TOKEN_TOTAL, MODEL_WIDTH))
    row_scale = jnp.exp(jax.random.uniform(keys_all[3], (TOKEN_TOTAL, 1), minval=0.0, maxval=math.log(10.0)))
    return (values_base * row_scale * column_scale[None, :]).astype(jnp.bfloat16)


def strengthened(result, stream_key, source, target, parts, factor):
    owner, partner = [(jnp.arange(result.shape[position]) // (result.shape[position] // parts)).reshape([-1 if axis == position else 1 for axis in range(result.ndim)]) for position in (source, target)]
    chosen = jax.random.permutation(stream_key, parts)[partner]
    strong = (owner == chosen) | (owner == (partner + parts // 2) % parts)
    return jnp.where(strong, factor * result, result)


def steps_of(key, extent, pieces, least, largest):
    loudness, own = 1.0, jax.random.fold_in(key, 6)
    for position, parts in pieces:
        heights = jnp.exp(jax.random.uniform(jax.random.fold_in(own, position), (parts,), jnp.float32, least / len(pieces), largest / len(pieces)))
        loudness = loudness * jnp.repeat(heights, extent[position] // parts).reshape([-1 if axis == position else 1 for axis in range(len(extent))])
    return loudness


def profile(count, total, reach, lean):
    weights = [(1 << 20) // math.isqrt(standing ** lean) + 1 for standing in range(2, count + 1)]
    spare, counts = total - reach - (count - 1), [1] * (count - 1)
    while spare > 0:
        movable = [i for i in range(count - 1) if counts[i] < reach]
        whole, left = sum([weights[i] for i in movable]), spare
        for i in movable:
            addition = min(reach - counts[i], max(1, left * weights[i] // whole), spare)
            counts[i] = counts[i] + addition
            spare = spare - addition
    return np.array([reach] + counts)


def uneven(own_key, amount, total, limit, slope):
    if amount == 2:
        one = jax.random.randint(own_key, (), max(1, total - limit), min(limit, total - 1) + 1)
        return jnp.stack([one, total - one])
    sizes = jnp.asarray(profile(amount, total, limit, slope), jnp.int32)
    twos = (amount - 1) // 2
    donor, taker = sizes[1:1 + 2 * twos:2], sizes[2:2 + 2 * twos:2]
    margin = jnp.minimum(donor - 1, limit - taker)
    shifted = jax.random.randint(jax.random.fold_in(own_key, 1), (twos,), 0, 1 << 20) % (margin + 1)
    sizes = sizes.at[1:1 + 2 * twos:2].set(donor - shifted).at[2:2 + 2 * twos:2].set(taker + shifted)
    return sizes[jax.random.permutation(jax.random.fold_in(own_key, 2), amount)]


def scatter_about(stream_key, shape, width, reach, cuts=(), held_as=jnp.bfloat16):
    level = steps_of(stream_key, shape, cuts, -0.22, 0.18) if cuts else 1.0
    array = jax.random.normal(stream_key, shape, jnp.float32) * width * level
    return jnp.minimum(jnp.maximum(array, -reach), reach).astype(held_as)


def bell_draw_with(stream_key, extent, scale, most, cuts, heavy, held_as=jnp.bfloat16):
    values = scale * jax.random.normal(stream_key, extent, jnp.float32)
    if cuts:
        values = values * steps_of(stream_key, extent, cuts, -0.22, 0.18)
    return jnp.clip(strengthened(values, jax.random.fold_in(stream_key, 3), *heavy), -most, most).astype(held_as)


def setup_inputs(seed: int = 0, part: int = 0) -> dict:
    key_of = jax.random.split(jax.random.key(seed), 9)
    part_keys = jax.random.split(jax.random.fold_in(key_of[8], part), 9)
    return {
        "hidden": draw_hidden(jax.random.fold_in(jax.random.fold_in(key_of[8], part), 71), part),
        "input_norm_scale": jnp.clip(1.0 + 0.15 * jax.random.normal(key_of[1], (MODEL_WIDTH,), jnp.float32), 0.25, 1.75).astype(jnp.bfloat16),
        "key_value_weight": bell_draw_with(key_of[2], (MODEL_WIDTH, 2, KEY_VALUE_WIDTH), MODEL_WIDTH ** -0.5, 0.09375, ((0, 4),), (0, 2, 4, 2.0)),
        "adapter_down_weight": scatter_about(part_keys[3], (ADAPTER_TOTAL, MODEL_WIDTH, 2 * ADAPTER_RANK), MODEL_WIDTH ** -0.5, 0.0625, ((0, 4), (1, 4))),
        "adapter_up_weight": scatter_about(part_keys[4], (ADAPTER_TOTAL, 2, ADAPTER_RANK, KEY_VALUE_WIDTH), ADAPTER_RANK ** -0.5, 0.75, ((0, 4),)),
        "request_adapter_index": draw_request_adapter_index(jax.random.fold_in(jax.random.fold_in(key_of[8], part), 71), part),
        "request_token_length": jax.vmap(lambda own: uneven(own, REQ_DEV, TOK_DEV, LONGEST_REQUEST, 2))(jax.random.split(part_keys[6], OWNERS)).reshape((OWNERS, REQ_DEV)).astype(jnp.int32),
        "adapter_storage_row": draw_adapter_storage_row(jax.random.fold_in(jax.random.fold_in(key_of[8], part), 71), part),
    }


def rotate_keys(head_keys, positions):
    half_dim = head_keys.shape[-1] // 2
    exponent = jnp.arange(half_dim, dtype=head_keys.dtype) * (2.0 / head_keys.shape[-1])
    frequency = jnp.exp(-exponent * math.log(10000.0))
    angles = positions.astype(head_keys.dtype)[:, None] * frequency[None, :]
    cosine = jnp.cos(angles)[:, None, :]
    sine_part = jnp.sin(angles)[:, None, :]
    first_half = head_keys[..., :half_dim]
    second_half = head_keys[..., half_dim:]
    return jnp.concatenate([first_half * cosine - second_half * sine_part, second_half * cosine + first_half * sine_part], axis=-1)

def token_positions(lengths, row_count):
    request_ends = jnp.cumsum(lengths).astype(jnp.int32)
    offsets = jnp.arange(row_count, dtype=jnp.int32)
    starts = lax.optimization_barrier(jnp.max(jnp.where(request_ends[None, :] <= offsets[:, None], request_ends[None, :], 0), axis=1)).astype(jnp.int32)
    return offsets - starts

def reference(hidden, input_norm_scale, key_value_weight, adapter_down_weight, adapter_up_weight, request_adapter_index, request_token_length, adapter_storage_row):
    widened = hidden.astype(jnp.float32)
    squares = lax.optimization_barrier(jnp.sum(widened * widened, axis=1, keepdims=True))
    normed = (widened * lax.rsqrt(squares / MODEL_WIDTH + 1e-05) * input_norm_scale.astype(jnp.float32)[None, :]).astype(jnp.bfloat16)
    plain_projection_sum = jnp.dot(normed, key_value_weight.reshape(MODEL_WIDTH, 2 * KEY_VALUE_WIDTH), preferred_element_type=jnp.float32).reshape(TOKEN_TOTAL, 2, KEY_VALUE_WIDTH)
    storage = adapter_storage_row[request_adapter_index].astype(jnp.int32)
    request_ends = jnp.cumsum(request_token_length, axis=1).astype(jnp.int32)
    device_start = (jnp.arange(OWNERS, dtype=jnp.int32) * TOK_DEV)[:, None]
    begins = (request_ends - request_token_length + device_start).reshape(-1).astype(jnp.int32)
    lengths = request_token_length.reshape(-1)
    padded = jnp.concatenate([normed, jnp.zeros((LONGEST_REQUEST, MODEL_WIDTH), jnp.bfloat16)], axis=0)
    keep_index = jnp.arange(LONGEST_REQUEST, dtype=jnp.int32)

    def accumulate_request(request, carried):
        start_row = begins[request]
        request_token_window = lax.dynamic_slice_in_dim(padded, start_row, LONGEST_REQUEST, 0)
        selected_adapter = storage[request]
        reduced_rank_product = jnp.dot(request_token_window, adapter_down_weight[selected_adapter], preferred_element_type=jnp.float32)
        reduced_rank_product = jnp.where((keep_index < lengths[request])[:, None], reduced_rank_product, jnp.zeros_like(reduced_rank_product))
        adapter_delta = jnp.einsum('sdp,dpe->sde', reduced_rank_product.reshape(LONGEST_REQUEST, 2, ADAPTER_RANK), adapter_up_weight[selected_adapter].astype(jnp.float32), precision=lax.Precision.HIGHEST)
        current = lax.dynamic_slice_in_dim(carried, start_row, LONGEST_REQUEST, 0)
        return lax.dynamic_update_slice_in_dim(carried, current + adapter_delta, start_row, 0)
    adapter_update_sum = lax.fori_loop(0, REQUEST_TOTAL, accumulate_request, jnp.zeros((TOKEN_TOTAL + LONGEST_REQUEST, 2, KEY_VALUE_WIDTH), jnp.float32))
    combined_output_sum = plain_projection_sum + adapter_update_sum[:TOKEN_TOTAL]

    def device_positions(lengths_row):
        return token_positions(lengths_row, TOK_DEV)
    positions = jax.vmap(device_positions)(request_token_length).reshape(-1)
    rotated = rotate_keys(combined_output_sum[:, 0, :].reshape(TOKEN_TOTAL, KVH, HD), positions)
    key_out = rotated.reshape(TOKEN_TOTAL, KEY_VALUE_WIDTH).astype(jnp.bfloat16)
    value_out = combined_output_sum[:, 1, :].astype(jnp.bfloat16)
    return (key_out, value_out)
```

```python
import functools
import math

import jax
import jax.numpy as jnp
from jax import lax
from jax.experimental import pallas as pl
from jax.experimental.pallas import tpu as pltpu
from jax.sharding import PartitionSpec as P

MODEL_WIDTH = 8192
HD = 128
CAP = 2
BLOCKS = 4
MESH = pl.DeviceIdType.MESH
F32 = jnp.float32
BF16 = jnp.bfloat16


def kernel(
    owners,
    ranks,
    rows_ref,
    tok_ref,
    freq_ref,
    scale_ref,
    h_hbm,
    w_hbm,
    a_hbm,
    b_hbm,
    key_ref,
    value_ref,
    hs,
    wv,
    av,
    bv,
    out_a,
    got_a,
    out_b,
    got_b,
    part,
    send,
    got_up,
    got_dn,
    low,
    low_send,
    low_got,
    ss,
    load_sem,
    w_sem,
    a_send_sem,
    a_sem,
    b_send_sem,
    b_sem,
    send_sem,
    up_sem,
    dn_sem,
    low_send_sem,
    low_sem,
    ss_send_sem,
    ss_sem,
):
    me = lax.axis_index("adapters")
    t = lax.axis_index("tensor")
    tokens, feats = hs.shape
    tb = tokens // BLOCKS
    cols = key_ref.shape[1]
    rank = bv.shape[2]
    last = ranks - 1
    is_lo = t == 0
    is_hi = t == last
    lower = t < ranks // 2

    def target(k):
        below = jnp.where(k < last - t, last - k, k - (last - t))
        above = jnp.where(k < t, k, last - (k - t))
        return jnp.where(k == last, t, jnp.where(lower, below, above))

    def rows(b):
        return pl.ds(pl.multiple_of(b * tb, tb), tb)

    h_copy = [
        pltpu.make_async_copy(h_hbm.at[rows(b)], hs.at[rows(b)], load_sem.at[2 + b])
        for b in range(BLOCKS)
    ]

    def w_copy(k):
        j = target(k)
        return pltpu.make_async_copy(
            w_hbm.at[:, :, pl.ds(pl.multiple_of(j * cols, 128), cols)], wv.at[j], w_sem.at[k]
        )

    a_copy = pltpu.make_async_copy(a_hbm, av, load_sem.at[0])
    b_copy = pltpu.make_async_copy(
        b_hbm.at[:, :, :, pl.ds(pl.multiple_of(t * cols, 128), cols)], bv, load_sem.at[1]
    )
    for b in range(BLOCKS):
        h_copy[b].start()
    w_copy(0).start()
    a_copy.start()
    b_copy.start()
    for k in range(1, ranks):
        w_copy(k).start()

    ss[...] = jnp.zeros_like(ss)
    got_b[...] = jnp.zeros_like(got_b)

    barrier = pltpu.get_barrier_semaphore()
    for k in range(1, owners):
        pl.semaphore_signal(
            barrier, inc=1, device_id={"adapters": lax.rem(me + k, owners)}, device_id_type=MESH
        )
    for k in range(1, ranks):
        pl.semaphore_signal(
            barrier, inc=1, device_id={"tensor": lax.rem(t + k, ranks)}, device_id_type=MESH
        )
    pl.semaphore_wait(barrier, owners - 1 + ranks - 1)

    def up_copy(j, b):
        return pltpu.make_async_remote_copy(
            src_ref=send.at[j, rows(b)],
            dst_ref=got_up.at[j, rows(b)],
            send_sem=send_sem.at[j, b],
            recv_sem=up_sem.at[j, b],
            device_id={"tensor": lax.rem(t + 1, ranks)},
            device_id_type=MESH,
        )

    def dn_copy(j, b):
        return pltpu.make_async_remote_copy(
            src_ref=send.at[j, rows(b)],
            dst_ref=got_dn.at[j, rows(b)],
            send_sem=send_sem.at[j, b],
            recv_sem=dn_sem.at[j, b],
            device_id={"tensor": lax.rem(t + last, ranks)},
            device_id_type=MESH,
        )

    def low_copy(way, b):
        return pltpu.make_async_remote_copy(
            src_ref=low_send.at[way, rows(b)],
            dst_ref=low_got.at[way, rows(b)],
            send_sem=low_send_sem.at[way, b],
            recv_sem=low_sem.at[way, b],
            device_id={"tensor": lax.rem(t + (1 if way == 0 else last), ranks)},
            device_id_type=MESH,
        )

    def ss_copy(k):
        return pltpu.make_async_remote_copy(
            src_ref=ss.at[t],
            dst_ref=ss.at[t],
            send_sem=ss_send_sem.at[k],
            recv_sem=ss_sem.at[t],
            device_id={"tensor": lax.rem(t + k, ranks)},
            device_id_type=MESH,
        )

    def ss_arrival(k):
        source = lax.rem(t + k, ranks)
        return pltpu.make_async_remote_copy(
            src_ref=ss.at[source],
            dst_ref=ss.at[source],
            send_sem=ss_send_sem.at[k],
            recv_sem=ss_sem.at[source],
            device_id={"tensor": source},
            device_id_type=MESH,
        )

    def a_move(k, source, s):
        d = lax.rem(me + k, owners)
        return pltpu.make_async_remote_copy(
            src_ref=out_a.at[k - 1, s],
            dst_ref=got_a.at[source * CAP + s],
            send_sem=a_send_sem.at[k, s],
            recv_sem=a_sem.at[source, s],
            device_id={"adapters": d},
            device_id_type=MESH,
        )

    def b_move(k, source, s, c):
        d = lax.rem(me + k, owners)
        return pltpu.make_async_remote_copy(
            src_ref=out_b.at[k - 1, s, c],
            dst_ref=got_b.at[
                source * CAP + s, pl.ds(c * rank, rank), pl.ds(c * cols, cols)
            ],
            send_sem=b_send_sem.at[k, s, c],
            recv_sem=b_sem.at[source, s, c],
            device_id={"adapters": d},
            device_id_type=MESH,
        )

    ones = jnp.ones((8, feats), BF16)
    contract = (((1,), (1,)), ((), ()))
    for b in range(BLOCKS):
        h_copy[b].wait()
    step = 128

    def prepare(i, carry):
        sl = pl.ds(pl.multiple_of(i * step, step), step)
        h = hs[sl, :].astype(F32)
        sq = h * h
        hi = sq.astype(BF16)
        lo = (sq - hi.astype(F32)).astype(BF16)
        total = lax.dot_general(ones, hi, contract, preferred_element_type=F32)
        total += lax.dot_general(ones, lo, contract, preferred_element_type=F32)
        ss[t, :, sl] = total
        hs[sl, :] = (h * scale_ref[...]).astype(BF16)
        return carry

    lax.fori_loop(0, tokens // step, prepare, 0)
    for k in range(1, ranks):
        ss_copy(k).start()

    def project(k):
        j = target(k)
        w_copy(k).wait()

        def one(b, carry):
            x = hs[rows(b), :]
            for c in range(2):
                y = jnp.dot(x, wv[j, c], preferred_element_type=F32)
                part[j, rows(b), pl.ds(c * cols, cols)] = y
                if k < last:

                    @pl.when(is_lo | is_hi)
                    def _():
                        send[j, rows(b), pl.ds(c * cols, cols)] = y.astype(BF16)

            if k < last:

                @pl.when(is_lo)
                def _():
                    up_copy(j, b).start()

                @pl.when(is_hi)
                def _():
                    dn_copy(j, b).start()

            return carry

        lax.fori_loop(0, BLOCKS, one, 0)

    project(0)

    a_copy.wait()
    b_copy.wait()
    piece = min(256, feats)
    order = sorted(range(1, owners), key=lambda k: abs(k - owners // 2))
    for k in order:
        d = lax.rem(me + k, owners)
        for s in range(CAP):
            row = rows_ref[d, s]

            def stage(i, carry):
                sl = pl.ds(pl.multiple_of(i * piece, piece), piece)
                out_a[k - 1, s, sl, :] = av[row, sl, :]
                return carry

            lax.fori_loop(0, feats // piece, stage, 0)
            a_move(k, me, s).start()
    for k in order:
        d = lax.rem(me + k, owners)
        for s in range(CAP):
            row = rows_ref[d, s]
            for c in range(2):
                out_b[k - 1, s, c] = bv[row, c]
                b_move(k, me, s, c).start()
    for s in range(CAP):
        row = rows_ref[me, s]

        def keep(i, carry):
            sl = pl.ds(pl.multiple_of(i * piece, piece), piece)
            got_a[me * CAP + s, sl, :] = av[row, sl, :]
            return carry

        lax.fori_loop(0, feats // piece, keep, 0)
        for c in range(2):
            got_b[me * CAP + s, pl.ds(c * rank, rank), pl.ds(c * cols, cols)] = bv[row, c]

    for k in range(1, ranks):
        project(k)

    def lowrank(slot, first):
        def one(b, carry):
            y = jnp.dot(hs[rows(b), :], got_a[slot], preferred_element_type=F32)
            y = jnp.where(tok_ref[rows(b), 0:1] == slot, y, 0.0)
            if first:
                low[rows(b), :] = y
            else:
                low[rows(b), :] = low[rows(b), :] + y
            return carry

        lax.fori_loop(0, BLOCKS, one, 0)

    for s in range(CAP):
        lowrank(me * CAP + s, s == 0)

    def forward(k):
        ju = last - k
        jd = k

        def one(b, carry):
            @pl.when((t > 0) & (ju > t))
            def _():
                up_copy(ju, b).wait_recv()

                @pl.when(t < last)
                def _():
                    send[ju, rows(b), :] = (
                        part[ju, rows(b), :] + got_up[ju, rows(b), :].astype(F32)
                    ).astype(BF16)
                    up_copy(ju, b).start()

            @pl.when((t < last) & (jd < t))
            def _():
                dn_copy(jd, b).wait_recv()

                @pl.when(t > 0)
                def _():
                    send[jd, rows(b), :] = (
                        part[jd, rows(b), :] + got_dn[jd, rows(b), :].astype(F32)
                    ).astype(BF16)
                    dn_copy(jd, b).start()

            return carry

        lax.fori_loop(0, BLOCKS, one, 0)

    for k in range(last):
        forward(k)

    arrivals = sorted(range(1, owners), key=lambda k: abs(k - owners // 2), reverse=True)
    for k in arrivals:
        source = lax.rem(me + owners - k, owners)
        for s in range(CAP):
            a_move(k, source, s).wait_recv()
            lowrank(source * CAP + s, False)

    def low_start(b, carry):
        mine = low[rows(b), :]

        @pl.when(t == 0)
        def _():
            low_send[0, rows(b), :] = mine.astype(BF16)
            low_copy(0, b).start()

        @pl.when(t == last)
        def _():
            low_send[1, rows(b), :] = mine.astype(BF16)
            low_copy(1, b).start()

        return carry

    lax.fori_loop(0, BLOCKS, low_start, 0)

    for b in range(BLOCKS):

        @pl.when(t > 0)
        def _():
            low_copy(0, b).wait_recv()

            @pl.when(t < last)
            def _():
                low_send[0, rows(b), :] = (
                    low[rows(b), :] + low_got[0, rows(b), :].astype(F32)
                ).astype(BF16)
                low_copy(0, b).start()

        @pl.when(t < last)
        def _():
            low_copy(1, b).wait_recv()

            @pl.when(t > 0)
            def _():
                low_send[1, rows(b), :] = (
                    low[rows(b), :] + low_got[1, rows(b), :].astype(F32)
                ).astype(BF16)
                low_copy(1, b).start()

    for k in range(1, ranks):
        ss_arrival(k).wait_recv()
    for k in arrivals:
        source = lax.rem(me + owners - k, owners)
        for s in range(CAP):
            for c in range(2):
                b_move(k, source, s, c).wait_recv()

    slots = owners * CAP

    def finish(b, carry):
        sl = rows(b)
        total = part[t, sl, :]
        lows = low[sl, :]

        gains = jnp.sum(ss[:, :, sl], axis=0).T[:, 0:1]
        gains = lax.rsqrt(gains * (1.0 / MODEL_WIDTH) + 1e-05)
        part[t, sl, :] = total

        @pl.when(t > 0)
        def _():
            up_copy(t, b).wait_recv()
            part[t, sl, :] = part[t, sl, :] + got_up[t, sl, :].astype(F32)
            low[sl, :] = low[sl, :] + low_got[0, sl, :].astype(F32)

        @pl.when(t < last)
        def _():
            dn_copy(t, b).wait_recv()
            part[t, sl, :] = part[t, sl, :] + got_dn[t, sl, :].astype(F32)
            low[sl, :] = low[sl, :] + low_got[1, sl, :].astype(F32)

        lows = low[sl, :]
        hi = lows.astype(BF16).astype(F32)
        lo = lows - hi
        mine = tok_ref[sl, 0:1]
        picked_hi = jnp.concatenate(
            [jnp.where(mine == s, hi, 0.0).astype(BF16) for s in range(slots)], axis=1
        )
        picked_lo = jnp.concatenate(
            [jnp.where(mine == s, lo, 0.0).astype(BF16) for s in range(slots)], axis=1
        )
        maps = got_b[...].reshape(slots * 2 * rank, 2 * cols)
        total = part[t, sl, :]
        total += jnp.dot(picked_hi, maps, preferred_element_type=F32)
        total += jnp.dot(picked_lo, maps, preferred_element_type=F32)
        total = total * gains
        value_ref[sl, :] = total[:, cols:].astype(BF16)
        angles = tok_ref[sl, 1:2].astype(F32) * freq_ref[...]
        cosine = jnp.cos(angles)
        sine = jnp.sin(angles)
        lane = lax.broadcasted_iota(jnp.int32, sine.shape, 1)
        sine = jnp.where(lane < HD // 2, -sine, sine)
        for head in range(cols // HD):
            x = total[:, head * HD : (head + 1) * HD]
            key_ref[sl, pl.ds(head * HD, HD)] = (
                x * cosine + pltpu.roll(x, HD // 2, 1) * sine
            ).astype(BF16)
        return carry

    lax.fori_loop(0, BLOCKS, finish, 0)

    for k in range(1, ranks):
        ss_copy(k).wait_send()
    for k in range(1, owners):
        for s in range(CAP):
            a_move(k, me, s).wait_send()
            for c in range(2):
                b_move(k, me, s, c).wait_send()

    def drain(b, carry):
        for j in range(ranks):

            @pl.when(j != t)
            def _():
                up_copy(j, b).wait_send()

        @pl.when(t < last)
        def _():
            low_copy(0, b).wait_send()

        @pl.when(t > 0)
        def _():
            low_copy(1, b).wait_send()

        return carry

    lax.fori_loop(0, BLOCKS, drain, 0)


def body(
    hidden,
    input_norm_scale,
    key_value_weight,
    adapter_down_weight,
    adapter_up_weight,
    request_adapter_index,
    request_token_length,
    adapter_storage_row,
):
    tokens, feats = hidden.shape
    requests = request_adapter_index.shape[0]
    stored = adapter_down_weight.shape[0]
    width = key_value_weight.shape[2]
    rank = adapter_up_weight.shape[2]
    owners = lax.axis_size("adapters")
    ranks = lax.axis_size("tensor")
    me = lax.axis_index("adapters")
    cols = width // ranks
    slots = owners * CAP

    id_table = jnp.arange(adapter_storage_row.shape[0], dtype=jnp.int32)

    def storage_rows(ids):
        return jnp.sum(jnp.where(ids[..., None] == id_table, adapter_storage_row, 0), axis=-1)

    every_row = storage_rows(
        lax.all_gather(request_adapter_index, "adapters", axis=0, tiled=True).reshape(
            owners, requests
        )
    )
    held_here = every_row // stored == me
    local = every_row % stored
    least = jnp.min(jnp.where(held_here, local, stored - 1), axis=1)
    most = jnp.max(jnp.where(held_here, local, 0), axis=1)
    wanted = jnp.stack([least, most], axis=1)

    own_row = storage_rows(request_adapter_index)
    own_owner = own_row // stored
    same = own_owner[:, None] == own_owner[None, :]
    own_least = jnp.min(jnp.where(same, own_row[None, :], slots * stored), axis=1)
    own_slot = own_owner * CAP + (own_row != own_least).astype(jnp.int32)
    lengths = request_token_length[0]
    ends = jnp.sum(
        jnp.where(jnp.arange(requests)[None, :] <= jnp.arange(requests)[:, None], lengths, 0),
        axis=1,
    )
    begins = ends - lengths
    offsets = jnp.arange(tokens, dtype=jnp.int32)[:, None]
    inside = (begins <= offsets) & (offsets < ends)
    token_slot = jnp.sum(jnp.where(inside, own_slot, 0), axis=1)
    token_position = jnp.sum(jnp.where(inside, offsets - begins, 0), axis=1)
    token_info = jnp.stack([token_slot, token_position], axis=1)
    half = HD // 2
    exponent = (jnp.arange(HD, dtype=jnp.int32) % half).astype(F32) * (2.0 / HD)
    frequency = jnp.exp(-exponent * math.log(10000.0))[None, :]
    scale = input_norm_scale.astype(F32)[None, :]
    weight = jnp.transpose(key_value_weight, (1, 0, 2))

    vmem = pl.BlockSpec(memory_space=pltpu.VMEM)
    smem = pl.BlockSpec(memory_space=pltpu.SMEM)
    anywhere = pl.BlockSpec(memory_space=pl.ANY)
    dma = pltpu.SemaphoreType.DMA
    return pl.pallas_call(
        functools.partial(kernel, owners, ranks),
        out_shape=(
            jax.ShapeDtypeStruct((tokens, cols), BF16),
            jax.ShapeDtypeStruct((tokens, cols), BF16),
        ),
        in_specs=[smem, vmem, vmem, vmem] + [anywhere] * 4,
        out_specs=(vmem, vmem),
        scratch_shapes=[
            pltpu.VMEM((tokens, feats), BF16),
            pltpu.VMEM((ranks, 2, feats, cols), BF16),
            pltpu.VMEM((stored, feats, 2 * rank), BF16),
            pltpu.VMEM((stored, 2, rank, cols), BF16),
            pltpu.VMEM((owners - 1, CAP, feats, 2 * rank), BF16),
            pltpu.VMEM((slots, feats, 2 * rank), BF16),
            pltpu.VMEM((owners - 1, CAP, 2, rank, cols), BF16),
            pltpu.VMEM((slots, 2 * rank, 2 * cols), BF16),
            pltpu.VMEM((ranks, tokens, 2 * cols), F32),
            pltpu.VMEM((ranks, tokens, 2 * cols), BF16),
            pltpu.VMEM((ranks, tokens, 2 * cols), BF16),
            pltpu.VMEM((ranks, tokens, 2 * cols), BF16),
            pltpu.VMEM((tokens, 2 * rank), F32),
            pltpu.VMEM((2, tokens, 2 * rank), BF16),
            pltpu.VMEM((2, tokens, 2 * rank), BF16),
            pltpu.VMEM((ranks, 8, tokens), F32),
            dma((2 + BLOCKS,)),
            dma((ranks,)),
            dma((owners, CAP)),
            dma((owners, CAP)),
            dma((owners, CAP, 2)),
            dma((owners, CAP, 2)),
            dma((ranks, BLOCKS)),
            dma((ranks, BLOCKS)),
            dma((ranks, BLOCKS)),
            dma((2, BLOCKS)),
            dma((2, BLOCKS)),
            dma((ranks,)),
            dma((ranks,)),
        ],
        compiler_params=pltpu.CompilerParams(
            collective_id=0, has_side_effects=True, vmem_limit_bytes=60 * 1024 * 1024
        ),
        cost_estimate=pl.CostEstimate(
            flops=2 * tokens * feats * (2 * width + slots * 2 * rank),
            bytes_accessed=20 * 1024 * 1024,
            transcendentals=0,
        ),
    )(
        wanted,
        token_info,
        frequency,
        scale,
        hidden,
        weight,
        adapter_down_weight,
        adapter_up_weight,
    )


def solution(mesh):
    placed = (
        P(("groups", "adapters"), "tensor"),
        P("tensor"),
        P("tensor", None, None),
        P(("groups", "adapters"), "tensor", None),
        P(("groups", "adapters"), None, None, None),
        P(("groups", "adapters")),
        P(("groups", "adapters"), None),
        P("groups"),
    )
    return jax.shard_map(
        body,
        mesh=mesh,
        in_specs=placed,
        out_specs=(P(("groups", "adapters"), "tensor"), P(("groups", "adapters"), "tensor")),
        check_vma=False,
    )
```

```python
import functools
import math

import jax
import jax.numpy as jnp
from jax import lax
from jax.experimental import pallas as pl
from jax.experimental.pallas import tpu as pltpu
from jax.sharding import PartitionSpec as P

MODEL_WIDTH = 8192
HD = 128
CAP = 2
BLOCKS = 4
MESH = pl.DeviceIdType.MESH
F32 = jnp.float32
BF16 = jnp.bfloat16


def kernel(
    owners,
    ranks,
    rows_ref,
    tok_ref,
    freq_ref,
    scale_ref,
    h_hbm,
    w_hbm,
    a_hbm,
    b_hbm,
    key_ref,
    value_ref,
    hs,
    wv,
    av,
    bv,
    out_a,
    got_a,
    out_b,
    got_b,
    part,
    send,
    got_up,
    got_dn,
    low,
    low_send,
    low_got,
    ss,
    slot_of,
    cosines,
    sines,
    load_sem,
    w_sem,
    a_send_sem,
    a_sem,
    b_send_sem,
    b_sem,
    send_sem,
    up_sem,
    dn_sem,
    low_send_sem,
    low_sem,
    ss_send_sem,
    ss_sem,
):
    me = lax.axis_index("adapters")
    t = lax.axis_index("tensor")
    tokens, feats = hs.shape
    tb = tokens // BLOCKS
    cols = key_ref.shape[1]
    rank = bv.shape[2]
    last = ranks - 1
    is_lo = t == 0
    is_hi = t == last
    lower = t < ranks // 2

    def target(k):
        below = jnp.where(k < last - t, last - k, k - (last - t))
        above = jnp.where(k < t, k, last - (k - t))
        return jnp.where(k == last, t, jnp.where(lower, below, above))

    def rows(b):
        return pl.ds(pl.multiple_of(b * tb, tb), tb)

    h_copy = [
        pltpu.make_async_copy(h_hbm.at[rows(b)], hs.at[rows(b)], load_sem.at[2 + b])
        for b in range(BLOCKS)
    ]

    def w_copy(k):
        j = target(k)
        return pltpu.make_async_copy(
            w_hbm.at[:, :, pl.ds(pl.multiple_of(j * cols, 128), cols)], wv.at[j], w_sem.at[k]
        )

    a_copy = pltpu.make_async_copy(a_hbm, av, load_sem.at[0])
    b_copy = pltpu.make_async_copy(
        b_hbm.at[:, :, :, pl.ds(pl.multiple_of(t * cols, 128), cols)], bv, load_sem.at[1]
    )
    for b in range(BLOCKS):
        h_copy[b].start()
    w_copy(0).start()
    a_copy.start()
    b_copy.start()
    for k in range(1, ranks):
        w_copy(k).start()

    ss[...] = jnp.zeros_like(ss)
    got_b[...] = jnp.zeros_like(got_b)

    barrier = pltpu.get_barrier_semaphore()
    for k in range(1, owners):
        pl.semaphore_signal(
            barrier, inc=1, device_id={"adapters": lax.rem(me + k, owners)}, device_id_type=MESH
        )
    for k in range(1, ranks):
        pl.semaphore_signal(
            barrier, inc=1, device_id={"tensor": lax.rem(t + k, ranks)}, device_id_type=MESH
        )
    pl.semaphore_wait(barrier, owners - 1 + ranks - 1)

    def up_copy(j, b):
        return pltpu.make_async_remote_copy(
            src_ref=send.at[j, rows(b)],
            dst_ref=got_up.at[j, rows(b)],
            send_sem=send_sem.at[j, b],
            recv_sem=up_sem.at[j, b],
            device_id={"tensor": lax.rem(t + 1, ranks)},
            device_id_type=MESH,
        )

    def dn_copy(j, b):
        return pltpu.make_async_remote_copy(
            src_ref=send.at[j, rows(b)],
            dst_ref=got_dn.at[j, rows(b)],
            send_sem=send_sem.at[j, b],
            recv_sem=dn_sem.at[j, b],
            device_id={"tensor": lax.rem(t + last, ranks)},
            device_id_type=MESH,
        )

    def low_copy(way, b):
        return pltpu.make_async_remote_copy(
            src_ref=low_send.at[way, rows(b)],
            dst_ref=low_got.at[way, rows(b)],
            send_sem=low_send_sem.at[way, b],
            recv_sem=low_sem.at[way, b],
            device_id={"tensor": lax.rem(t + (1 if way == 0 else last), ranks)},
            device_id_type=MESH,
        )

    def ss_copy(k):
        return pltpu.make_async_remote_copy(
            src_ref=ss.at[t],
            dst_ref=ss.at[t],
            send_sem=ss_send_sem.at[k],
            recv_sem=ss_sem.at[t],
            device_id={"tensor": lax.rem(t + k, ranks)},
            device_id_type=MESH,
        )

    def ss_arrival(k):
        source = lax.rem(t + k, ranks)
        return pltpu.make_async_remote_copy(
            src_ref=ss.at[source],
            dst_ref=ss.at[source],
            send_sem=ss_send_sem.at[k],
            recv_sem=ss_sem.at[source],
            device_id={"tensor": source},
            device_id_type=MESH,
        )

    def a_move(k, source, s):
        d = lax.rem(me + k, owners)
        return pltpu.make_async_remote_copy(
            src_ref=out_a.at[k - 1, s],
            dst_ref=got_a.at[source * CAP + s],
            send_sem=a_send_sem.at[k, s],
            recv_sem=a_sem.at[source, s],
            device_id={"adapters": d},
            device_id_type=MESH,
        )

    def b_move(k, source, s, c):
        d = lax.rem(me + k, owners)
        return pltpu.make_async_remote_copy(
            src_ref=out_b.at[k - 1, s, c],
            dst_ref=got_b.at[
                source * CAP + s, pl.ds(c * rank, rank), pl.ds(c * cols, cols)
            ],
            send_sem=b_send_sem.at[k, s, c],
            recv_sem=b_sem.at[source, s, c],
            device_id={"adapters": d},
            device_id_type=MESH,
        )

    ones = jnp.ones((8, 128), BF16)
    contract = (((1,), (1,)), ((), ()))
    for b in range(BLOCKS):
        h_copy[b].wait()
    step = 128

    def prepare(i, carry):
        sl = pl.ds(pl.multiple_of(i * step, step), step)
        h = hs[sl, :].astype(F32)
        sq = h[:, :128] * h[:, :128]
        for c in range(1, feats // 128):
            sq += h[:, c * 128 : (c + 1) * 128] * h[:, c * 128 : (c + 1) * 128]
        hi = sq.astype(BF16)
        lo = (sq - hi.astype(F32)).astype(BF16)
        total = lax.dot_general(ones, hi, contract, preferred_element_type=F32)
        total += lax.dot_general(ones, lo, contract, preferred_element_type=F32)
        ss[t, :, sl] = total
        hs[sl, :] = (h * scale_ref[...]).astype(BF16)
        return carry

    lax.fori_loop(0, tokens // step, prepare, 0)
    for k in range(1, ranks):
        ss_copy(k).start()

    def project(k):
        j = target(k)
        w_copy(k).wait()

        def one(b, carry):
            x = hs[rows(b), :]
            for c in range(2):
                y = jnp.dot(x, wv[j, c], preferred_element_type=F32)
                part[j, rows(b), pl.ds(c * cols, cols)] = y
                if k < last:

                    @pl.when(is_lo | is_hi)
                    def _():
                        send[j, rows(b), pl.ds(c * cols, cols)] = y.astype(BF16)

            if k < last:

                @pl.when(is_lo)
                def _():
                    up_copy(j, b).start()

                @pl.when(is_hi)
                def _():
                    dn_copy(j, b).start()

            return carry

        lax.fori_loop(0, BLOCKS, one, 0)

    project(0)

    a_copy.wait()
    b_copy.wait()
    piece = min(256, feats)
    order = sorted(range(1, owners), key=lambda k: abs(k - owners // 2))
    for k in order:
        d = lax.rem(me + k, owners)
        for s in range(CAP):
            row = rows_ref[d, s]

            def stage(i, carry):
                sl = pl.ds(pl.multiple_of(i * piece, piece), piece)
                out_a[k - 1, s, sl, :] = av[row, sl, :]
                return carry

            lax.fori_loop(0, feats // piece, stage, 0)
            a_move(k, me, s).start()
    for k in order:
        d = lax.rem(me + k, owners)
        for s in range(CAP):
            row = rows_ref[d, s]
            for c in range(2):
                out_b[k - 1, s, c] = bv[row, c]
                b_move(k, me, s, c).start()
    for s in range(CAP):
        row = rows_ref[me, s]

        def keep(i, carry):
            sl = pl.ds(pl.multiple_of(i * piece, piece), piece)
            got_a[me * CAP + s, sl, :] = av[row, sl, :]
            return carry

        lax.fori_loop(0, feats // piece, keep, 0)
        for c in range(2):
            got_b[me * CAP + s, pl.ds(c * rank, rank), pl.ds(c * cols, cols)] = bv[row, c]

    for k in range(1, ranks):
        project(k)

    lane = lax.broadcasted_iota(jnp.int32, (step, HD), 1)

    def describe(i, carry):
        sl = pl.ds(pl.multiple_of(i * step, step), step)
        slot_of[sl, :] = jnp.broadcast_to(tok_ref[sl, 0:1], (step, HD))
        angles = tok_ref[sl, 1:2].astype(F32) * freq_ref[...]
        cosines[sl, :] = jnp.cos(angles)
        sine = jnp.sin(angles)
        sines[sl, :] = jnp.where(lane < HD // 2, -sine, sine)
        return carry

    lax.fori_loop(0, tokens // step, describe, 0)

    def lowrank(source, first):
        def one(b, carry):
            maps = jnp.concatenate([got_a[source * CAP], got_a[source * CAP + 1]], axis=1)
            y = jnp.dot(hs[rows(b), :], maps, preferred_element_type=F32)
            slot = slot_of[rows(b), :]
            picked = jnp.where(slot == source * CAP, y[:, : 2 * rank], 0.0)
            picked += jnp.where(slot == source * CAP + 1, y[:, 2 * rank :], 0.0)
            if first:
                low[rows(b), :] = picked
            else:
                low[rows(b), :] = low[rows(b), :] + picked
            return carry

        lax.fori_loop(0, BLOCKS, one, 0)

    lowrank(me, True)

    def forward(k):
        ju = last - k
        jd = k

        def one(b, carry):
            @pl.when((t > 0) & (ju > t))
            def _():
                up_copy(ju, b).wait_recv()

                @pl.when(t < last)
                def _():
                    send[ju, rows(b), :] = (
                        part[ju, rows(b), :] + got_up[ju, rows(b), :].astype(F32)
                    ).astype(BF16)
                    up_copy(ju, b).start()

            @pl.when((t < last) & (jd < t))
            def _():
                dn_copy(jd, b).wait_recv()

                @pl.when(t > 0)
                def _():
                    send[jd, rows(b), :] = (
                        part[jd, rows(b), :] + got_dn[jd, rows(b), :].astype(F32)
                    ).astype(BF16)
                    dn_copy(jd, b).start()

            return carry

        lax.fori_loop(0, BLOCKS, one, 0)

    for k in range(last):
        forward(k)

    arrivals = sorted(range(1, owners), key=lambda k: abs(k - owners // 2), reverse=True)
    for k in arrivals:
        source = lax.rem(me + owners - k, owners)
        for s in range(CAP):
            a_move(k, source, s).wait_recv()
        lowrank(source, False)

    def low_start(b, carry):
        mine = low[rows(b), :]

        @pl.when(t == 0)
        def _():
            low_send[0, rows(b), :] = mine.astype(BF16)
            low_copy(0, b).start()

        @pl.when(t == last)
        def _():
            low_send[1, rows(b), :] = mine.astype(BF16)
            low_copy(1, b).start()

        return carry

    lax.fori_loop(0, BLOCKS, low_start, 0)

    for b in range(BLOCKS):

        @pl.when(t > 0)
        def _():
            low_copy(0, b).wait_recv()

            @pl.when(t < last)
            def _():
                low_send[0, rows(b), :] = (
                    low[rows(b), :] + low_got[0, rows(b), :].astype(F32)
                ).astype(BF16)
                low_copy(0, b).start()

        @pl.when(t < last)
        def _():
            low_copy(1, b).wait_recv()

            @pl.when(t > 0)
            def _():
                low_send[1, rows(b), :] = (
                    low[rows(b), :] + low_got[1, rows(b), :].astype(F32)
                ).astype(BF16)
                low_copy(1, b).start()

    for k in range(1, ranks):
        ss_arrival(k).wait_recv()
    for k in arrivals:
        source = lax.rem(me + owners - k, owners)
        for s in range(CAP):
            for c in range(2):
                b_move(k, source, s, c).wait_recv()

    slots = owners * CAP

    def lift(b, carry):
        sl = rows(b)

        @pl.when(t > 0)
        def _():
            low[sl, :] = low[sl, :] + low_got[0, sl, :].astype(F32)

        @pl.when(t < last)
        def _():
            low[sl, :] = low[sl, :] + low_got[1, sl, :].astype(F32)

        lows = low[sl, :]
        hi = lows.astype(BF16).astype(F32)
        lo = lows - hi
        slot = slot_of[sl, :]
        maps = got_b[...].reshape(slots * 2 * rank, 2 * cols)
        total = part[t, sl, :]
        for term in (hi, lo):
            picked = jnp.concatenate(
                [jnp.where(slot == s, term, 0.0).astype(BF16) for s in range(slots)], axis=1
            )
            total += jnp.dot(picked, maps, preferred_element_type=F32)
        part[t, sl, :] = total
        return carry

    lax.fori_loop(0, BLOCKS, lift, 0)

    def finish(b, carry):
        sl = rows(b)
        gains = jnp.sum(ss[:, :, sl], axis=0).T[:, 0:1]
        gains = lax.rsqrt(gains * (1.0 / MODEL_WIDTH) + 1e-05)

        @pl.when(t > 0)
        def _():
            up_copy(t, b).wait_recv()
            part[t, sl, :] = part[t, sl, :] + got_up[t, sl, :].astype(F32)

        @pl.when(t < last)
        def _():
            dn_copy(t, b).wait_recv()
            part[t, sl, :] = part[t, sl, :] + got_dn[t, sl, :].astype(F32)

        total = part[t, sl, :] * gains
        value_ref[sl, :] = total[:, cols:].astype(BF16)
        for head in range(cols // HD):
            x = total[:, head * HD : (head + 1) * HD]
            key_ref[sl, pl.ds(head * HD, HD)] = (
                x * cosines[sl, :] + pltpu.roll(x, HD // 2, 1) * sines[sl, :]
            ).astype(BF16)
        return carry

    lax.fori_loop(0, BLOCKS, finish, 0)

    for k in range(1, ranks):
        ss_copy(k).wait_send()
    for k in range(1, owners):
        for s in range(CAP):
            a_move(k, me, s).wait_send()
            for c in range(2):
                b_move(k, me, s, c).wait_send()

    def drain(b, carry):
        for j in range(ranks):

            @pl.when(j != t)
            def _():
                up_copy(j, b).wait_send()

        @pl.when(t < last)
        def _():
            low_copy(0, b).wait_send()

        @pl.when(t > 0)
        def _():
            low_copy(1, b).wait_send()

        return carry

    lax.fori_loop(0, BLOCKS, drain, 0)


def body(
    hidden,
    input_norm_scale,
    key_value_weight,
    adapter_down_weight,
    adapter_up_weight,
    request_adapter_index,
    request_token_length,
    adapter_storage_row,
):
    tokens, feats = hidden.shape
    requests = request_adapter_index.shape[0]
    stored = adapter_down_weight.shape[0]
    width = key_value_weight.shape[2]
    rank = adapter_up_weight.shape[2]
    owners = lax.axis_size("adapters")
    ranks = lax.axis_size("tensor")
    me = lax.axis_index("adapters")
    cols = width // ranks
    slots = owners * CAP

    id_table = jnp.arange(adapter_storage_row.shape[0], dtype=jnp.int32)

    def storage_rows(ids):
        return jnp.sum(jnp.where(ids[..., None] == id_table, adapter_storage_row, 0), axis=-1)

    every_row = storage_rows(
        lax.all_gather(request_adapter_index, "adapters", axis=0, tiled=True).reshape(
            owners, requests
        )
    )
    held_here = every_row // stored == me
    local = every_row % stored
    least = jnp.min(jnp.where(held_here, local, stored - 1), axis=1)
    most = jnp.max(jnp.where(held_here, local, 0), axis=1)
    wanted = jnp.stack([least, most], axis=1)

    own_row = storage_rows(request_adapter_index)
    own_owner = own_row // stored
    same = own_owner[:, None] == own_owner[None, :]
    own_least = jnp.min(jnp.where(same, own_row[None, :], slots * stored), axis=1)
    own_slot = own_owner * CAP + (own_row != own_least).astype(jnp.int32)
    lengths = request_token_length[0]
    ends = jnp.sum(
        jnp.where(jnp.arange(requests)[None, :] <= jnp.arange(requests)[:, None], lengths, 0),
        axis=1,
    )
    begins = ends - lengths
    offsets = jnp.arange(tokens, dtype=jnp.int32)[:, None]
    inside = (begins <= offsets) & (offsets < ends)
    token_slot = jnp.sum(jnp.where(inside, own_slot, 0), axis=1)
    token_position = jnp.sum(jnp.where(inside, offsets - begins, 0), axis=1)
    token_info = jnp.stack([token_slot, token_position], axis=1)
    half = HD // 2
    exponent = (jnp.arange(HD, dtype=jnp.int32) % half).astype(F32) * (2.0 / HD)
    frequency = jnp.exp(-exponent * math.log(10000.0))[None, :]
    scale = input_norm_scale.astype(F32)[None, :]
    weight = jnp.transpose(key_value_weight, (1, 0, 2))

    vmem = pl.BlockSpec(memory_space=pltpu.VMEM)
    smem = pl.BlockSpec(memory_space=pltpu.SMEM)
    anywhere = pl.BlockSpec(memory_space=pl.ANY)
    dma = pltpu.SemaphoreType.DMA
    return pl.pallas_call(
        functools.partial(kernel, owners, ranks),
        out_shape=(
            jax.ShapeDtypeStruct((tokens, cols), BF16),
            jax.ShapeDtypeStruct((tokens, cols), BF16),
        ),
        in_specs=[smem, vmem, vmem, vmem] + [anywhere] * 4,
        out_specs=(vmem, vmem),
        scratch_shapes=[
            pltpu.VMEM((tokens, feats), BF16),
            pltpu.VMEM((ranks, 2, feats, cols), BF16),
            pltpu.VMEM((stored, feats, 2 * rank), BF16),
            pltpu.VMEM((stored, 2, rank, cols), BF16),
            pltpu.VMEM((owners - 1, CAP, feats, 2 * rank), BF16),
            pltpu.VMEM((slots, feats, 2 * rank), BF16),
            pltpu.VMEM((owners - 1, CAP, 2, rank, cols), BF16),
            pltpu.VMEM((slots, 2 * rank, 2 * cols), BF16),
            pltpu.VMEM((ranks, tokens, 2 * cols), F32),
            pltpu.VMEM((ranks, tokens, 2 * cols), BF16),
            pltpu.VMEM((ranks, tokens, 2 * cols), BF16),
            pltpu.VMEM((ranks, tokens, 2 * cols), BF16),
            pltpu.VMEM((tokens, 2 * rank), F32),
            pltpu.VMEM((2, tokens, 2 * rank), BF16),
            pltpu.VMEM((2, tokens, 2 * rank), BF16),
            pltpu.VMEM((ranks, 8, tokens), F32),
            pltpu.VMEM((tokens, HD), jnp.int32),
            pltpu.VMEM((tokens, HD), F32),
            pltpu.VMEM((tokens, HD), F32),
            dma((2 + BLOCKS,)),
            dma((ranks,)),
            dma((owners, CAP)),
            dma((owners, CAP)),
            dma((owners, CAP, 2)),
            dma((owners, CAP, 2)),
            dma((ranks, BLOCKS)),
            dma((ranks, BLOCKS)),
            dma((ranks, BLOCKS)),
            dma((2, BLOCKS)),
            dma((2, BLOCKS)),
            dma((ranks,)),
            dma((ranks,)),
        ],
        compiler_params=pltpu.CompilerParams(
            collective_id=0, has_side_effects=True, vmem_limit_bytes=60 * 1024 * 1024
        ),
        cost_estimate=pl.CostEstimate(
            flops=2 * tokens * feats * (2 * width + slots * 2 * rank),
            bytes_accessed=20 * 1024 * 1024,
            transcendentals=0,
        ),
    )(
        wanted,
        token_info,
        frequency,
        scale,
        hidden,
        weight,
        adapter_down_weight,
        adapter_up_weight,
    )


def solution(mesh):
    placed = (
        P(("groups", "adapters"), "tensor"),
        P("tensor"),
        P("tensor", None, None),
        P(("groups", "adapters"), "tensor", None),
        P(("groups", "adapters"), None, None, None),
        P(("groups", "adapters")),
        P(("groups", "adapters"), None),
        P("groups"),
    )
    return jax.shard_map(
        body,
        mesh=mesh,
        in_specs=placed,
        out_specs=(P(("groups", "adapters"), "tensor"), P(("groups", "adapters"), "tensor")),
        check_vma=False,
    )
```
